512 devices in a mesh: ctx: 16 (over y, x_hi, core), cand: 32 (over z, x_lo).
Axes of the slice: x: 4 (x_hi: 2, x_lo: 2; x = x_hi * 2 + x_lo), y: 4, z: 16, core: 2. Of those that a mesh axis runs over, the one named last changes fastest.
Arguments:
- queries: bfloat16 [32, 128, 8192], P('cand', None, 'ctx'), may hold values from -4 to 4
- suffix_keys: bfloat16 [32, 128, 1024], P('cand'), may hold values from -10 to 10
- suffix_values: bfloat16 [32, 128, 1024], P('cand'), may hold values from -6 to 6
- prefix_keys: bfloat16 [16384, 1024], P('ctx'), may hold values from -9 to 9
- prefix_values: bfloat16 [16384, 1024], P('ctx'), may hold values from -6 to 6
- lengths: int32 [32], P('cand'), may hold values from 32 to 128, as said below
Outputs:
- attended: bfloat16 [32, 128, 8192], P('cand', None, 'ctx')
The draws below stay inside these ranges and needn't reach their ends.
Inputs may be any that keep to these rules, and one draw needn't show every extreme that they name: `lengths`: one candidate has exactly 128 live tokens.
All inputs are finite; a program needn't handle non-finite values.
Results may differ from the reference program's by a relative error of at most 0.0055.
Values may be sent and summed in bfloat16 or wider, within the bound.
A program may use at most 64 MiB of HBM per device.

```python
import math
import jax
import jax.numpy as jnp
from jax import lax

H = 64
KVH = 8
HD = 128
LS = 128
P_DEV = 1024
CANDS = 32
PREFIX = 16384
N_CTX = 16


def draw_queries(key, part):
    local = jax.random.fold_in(key, 1)
    full = jnp.clip(jax.random.normal(local, (CANDS, LS, H, HD), jnp.float32), -4.0, 4.0)
    return full.reshape(CANDS, LS, H * HD).astype(jnp.bfloat16)


def draw_prefix_keys(key, part):
    local = jax.random.fold_in(key, 2)
    full = jnp.clip(1.4 * jax.random.normal(local, (PREFIX, KVH, HD), jnp.float32), -9.0, 9.0)
    return full.reshape(PREFIX, KVH * HD).astype(jnp.bfloat16)


def draw_lengths(key, part):
    local = jax.random.fold_in(key, 3)
    first, second = jax.random.split(local)
    sizes = jax.random.randint(first, (CANDS,), LS // 4, LS + 1, dtype=jnp.int32)
    longest = jax.random.randint(second, (), 0, CANDS, dtype=jnp.int32)
    return jnp.where(jnp.arange(CANDS, dtype=jnp.int32) == longest, LS, sizes).astype(jnp.int32)


def steps_of(own_key, dims, pieces, low, largest):
    gain = 1.0
    for dim, blocks in pieces:
        draws = jax.random.uniform(jax.random.fold_in(jax.random.fold_in(own_key, 6), dim), (blocks,), jnp.float32, low / len(pieces), largest / len(pieces))
        gain = gain * jnp.repeat(jnp.exp(draws), dims[dim] // blocks).reshape((-1,) + (1,) * (len(dims) - 1 - dim))
    return gain


def centred(rng, extent, deviation, most, cuts=(), held_as=jnp.bfloat16):
    values = deviation * jax.random.normal(rng, extent, jnp.float32)
    if cuts:
        values = values * steps_of(rng, extent, cuts, -0.22, 0.18)
    return jnp.clip(values, -most, most).astype(held_as)


def setup_inputs(seed: int = 0) -> dict:
    streams_of = jax.random.split(jax.random.key(seed), 7)
    return {
        "queries": draw_queries(jax.random.fold_in(streams_of[6], 71), 0),
        "suffix_keys": centred(streams_of[1], (CANDS, LS, KVH * HD), 2.5, 10.0, ((0, 32),)),
        "suffix_values": centred(streams_of[2], (CANDS, LS, KVH * HD), 1.0, 6.0, ((0, 32),)),
        "prefix_keys": draw_prefix_keys(jax.random.fold_in(streams_of[6], 71), 0),
        "prefix_values": centred(streams_of[4], (PREFIX, KVH * HD), 1.0, 6.0, ((0, 16),)),
        "lengths": draw_lengths(jax.random.fold_in(streams_of[6], 71), 0),
    }


def block_part(groups, key_rows, value_rows):
    inv_root = 1.0 / math.sqrt(HD)
    scores = jnp.einsum('tkgd,pkd->tkgp', groups.astype(jnp.float32), key_rows.astype(jnp.float32)) * inv_root
    peak = lax.optimization_barrier(jnp.max(scores, axis=-1))
    weights = jnp.exp(scores - peak[..., None])
    block_sum = lax.optimization_barrier(jnp.sum(weights, axis=-1))
    rounded = lax.optimization_barrier(weights.astype(jnp.bfloat16))
    numerator = jnp.einsum('tkgp,pkd->tkgd', rounded.astype(jnp.float32), value_rows.astype(jnp.float32))
    partial_value = (numerator / block_sum[..., None]).astype(jnp.bfloat16)
    return (peak.reshape(LS, H), block_sum.reshape(LS, H), partial_value.reshape(LS, H, HD))

def reference(queries, suffix_keys, suffix_values, prefix_keys, prefix_values, lengths):
    inv_root = 1.0 / math.sqrt(HD)
    shard_keys = prefix_keys.reshape(N_CTX, P_DEV, KVH, HD)
    shard_values = prefix_values.reshape(N_CTX, P_DEV, KVH, HD)
    positions = jnp.arange(LS, dtype=jnp.int32)
    causal = positions[None, :] <= positions[:, None]

    def candidate(inputs):
        query_rows, key_rows, value_rows, length = inputs
        groups = query_rows.reshape(LS, KVH, H // KVH, HD)

        def one_block(pair):
            return block_part(groups, pair[0], pair[1])
        peaks, sums, partials = lax.map(one_block, (shard_keys, shard_values))
        partials = lax.optimization_barrier(partials)
        suffix_k = key_rows.reshape(LS, KVH, HD).astype(jnp.float32)
        suffix_v = value_rows.reshape(LS, KVH, HD).astype(jnp.float32)
        scores = jnp.einsum('tkgd,ukd->tkgu', groups.astype(jnp.float32), suffix_k) * inv_root
        scores = jnp.where(causal[:, None, None, :], scores, -jnp.inf)
        suffix_peak = lax.optimization_barrier(jnp.max(scores, axis=-1))
        weights = jnp.exp(scores - suffix_peak[..., None])
        suffix_sum = lax.optimization_barrier(jnp.sum(weights, axis=-1))
        rounded = lax.optimization_barrier(weights.astype(jnp.bfloat16))
        suffix_numerator = jnp.einsum('tkgu,ukd->tkgd', rounded.astype(jnp.float32), suffix_v)
        suffix_peak = suffix_peak.reshape(LS, H)
        suffix_sum = suffix_sum.reshape(LS, H)
        suffix_numerator = suffix_numerator.reshape(LS, H, HD)
        highest = jnp.maximum(lax.optimization_barrier(jnp.max(peaks, axis=0)), suffix_peak)
        block_weights = jnp.exp(peaks - highest) * sums
        own_weight = jnp.exp(suffix_peak - highest)
        numerator = lax.optimization_barrier(jnp.sum(block_weights[..., None] * partials.astype(jnp.float32), axis=0)) + own_weight[..., None] * suffix_numerator
        denominator = lax.optimization_barrier(jnp.sum(block_weights, axis=0)) + own_weight * suffix_sum
        mixed = numerator / denominator[..., None]
        active = (positions < length)[:, None, None]
        mixed = jnp.where(active, mixed, 0.0)
        return mixed.reshape(LS, H * HD).astype(jnp.bfloat16)
    return lax.map(candidate, (queries, suffix_keys, suffix_values, lengths))
```

```python
import functools
import math

import jax
import jax.numpy as jnp
from jax import lax
from jax.experimental import pallas as pl
from jax.experimental.pallas import tpu as pltpu
from jax.sharding import PartitionSpec as P

H = 64
KVH = 8
HD = 128
LS = 128
P_DEV = 1024
NY = 4
HERE = 4
W = HERE * LS
ONES = 8

MESH = pl.DeviceIdType.MESH
NT = (((1,), (1,)), ((), ()))
TN = (((0,), (0,)), ((), ()))
SCALE = math.log2(math.e) / math.sqrt(HD)
F32 = jnp.float32
BF16 = jnp.bfloat16


def place():
    ctx, cand = lax.axis_index("ctx"), lax.axis_index("cand")
    return ctx // 4, (ctx // 2) % 2, ctx % 2, cand // 2, cand % 2


def device(y, half, core, z, low):
    return {"ctx": (y * 2 + half) * 2 + core, "cand": z * 2 + low}


def heads_in_rows(block):
    return jnp.concatenate([block[:, i * HD : (i + 1) * HD] for i in range(HERE)], axis=0)


def kernel(
    q_hbm, sk_hbm, sv_hbm, pk_hbm, pv_hbm, len_ref, out_ref,
    own_q, suffix_k, suffix_v, keys, values, values_t, queries, parts, part_stats, got, got_stats,
    suffix_sum, suffix_stats,
    own_sem, kv_sem, kv_send, kv_recv, q_sem, q_send, q_recv, o_send, o_recv, s_send, s_recv,
):
    y, half, core, z, low = place()
    half_c, low_c = (half + core) % 2, (low + core) % 2

    head = y * 2 + half
    columns = pl.ds(pl.multiple_of(head * HD, HD), HD)
    own_copies = [
        pltpu.make_async_copy(q_hbm, own_q, own_sem.at[0]),
        pltpu.make_async_copy(sk_hbm.at[:, columns], suffix_k, own_sem.at[1]),
        pltpu.make_async_copy(sv_hbm.at[:, columns], suffix_v, own_sem.at[2]),
    ]
    for copy in own_copies:
        copy.start()

    def order(i):
        return (y + jnp.where(i < 2, i, 5 - i)) % NY

    rows = pl.ds(pl.multiple_of(core * P_DEV, P_DEV), P_DEV)

    def kv_columns(item, parity):
        return pl.ds(pl.multiple_of((item * 2 + parity) * HD, HD), HD)

    def kv_local(item, j):
        src, dst = ((pk_hbm, keys), (pv_hbm, values))[j]
        return pltpu.make_async_copy(
            src.at[:, kv_columns(item, half_c)], dst.at[item, rows, :], kv_sem.at[item, j]
        )

    def kv_remote(item, j):
        src, dst = ((pk_hbm, keys), (pv_hbm, values))[j]
        return pltpu.make_async_remote_copy(
            src_ref=src.at[:, kv_columns(item, 1 - half_c)],
            dst_ref=dst.at[item, rows, :],
            send_sem=kv_send.at[item, j],
            recv_sem=kv_recv.at[item, j],
            device_id=device(y, half, 1 - core, z, low),
            device_id_type=MESH,
        )

    for i in range(NY):
        for j in range(2):
            kv_local(order(i), j).start()

    barrier = pltpu.get_barrier_semaphore()
    for dy in range(NY):
        for other in range(2):
            for c in range(2):
                if (dy, other, c) == (0, 0, 0):
                    continue
                pl.semaphore_signal(
                    barrier,
                    inc=1,
                    device_id=device(
                        (y + dy) % NY, (half + other) % 2, (core + c) % 2, z, (low + other) % 2
                    ),
                    device_id_type=MESH,
                )
    for copy in own_copies:
        copy.wait()
    pl.semaphore_wait(barrier, 15)

    def q_copy(dy, other):
        return pltpu.make_async_remote_copy(
            src_ref=own_q,
            dst_ref=queries.at[y, core],
            send_sem=q_send.at[dy, other],
            recv_sem=q_recv.at[y, core],
            device_id=device((y + dy) % NY, (half + other) % 2, other, z, (low + other) % 2),
            device_id_type=MESH,
        )

    q_local = pltpu.make_async_copy(q_hbm, queries.at[y, 0], q_sem)

    @pl.when(core == 0)
    def _():
        q_local.start()

    @pl.when(core == 1)
    def _():
        q_copy(0, 0).start()

    for j in range(2):
        kv_remote(order(0), j).start()
    q_copy(0, 1).start()
    for dy in (1, 3, 2):
        q_copy(dy, 0).start()
        q_copy(dy, 1).start()
    for i in range(1, NY):
        for j in range(2):
            kv_remote(order(i), j).start()

    q_rows = heads_in_rows(own_q[...])
    scores = lax.dot_general(suffix_k[...], q_rows, NT, preferred_element_type=F32)
    u = lax.broadcasted_iota(jnp.int32, (LS, W), 0)
    t = lax.broadcasted_iota(jnp.int32, (LS, W), 1) % LS
    scores = jnp.where(u <= t, scores, -1e30)
    peak = jnp.max(scores, axis=0, keepdims=True)
    probs = jnp.exp2((scores - peak) * SCALE)
    total = jnp.sum(probs, axis=0, keepdims=True)
    suffix_sum[...] = lax.dot_general(
        suffix_v[...], probs.astype(BF16), TN, preferred_element_type=F32
    )
    for i in range(HERE):
        suffix_stats[i : i + 1, :] = peak[:, i * LS : (i + 1) * LS]
        suffix_stats[HERE + i : HERE + i + 1, :] = total[:, i * LS : (i + 1) * LS]

    values_t[HD:, :] = jnp.ones((ONES, 2 * P_DEV), BF16)

    def out_copy(item, c):
        return pltpu.make_async_remote_copy(
            src_ref=parts.at[item, c],
            dst_ref=got.at[y * 2 + core],
            send_sem=o_send.at[item, c],
            recv_sem=o_recv.at[y * 2 + core],
            device_id=device(item, half_c, c, z, low_c),
            device_id_type=MESH,
        )

    def stat_copy(item, c):
        return pltpu.make_async_remote_copy(
            src_ref=part_stats.at[item, c],
            dst_ref=got_stats.at[y * 2 + core],
            send_sem=s_send.at[item, c],
            recv_sem=s_recv.at[y * 2 + core],
            device_id=device(item, half_c, c, z, low_c),
            device_id_type=MESH,
        )

    def one_item(i, carry):
        item = order(i)
        for j in range(2):
            kv_local(item, j).wait()
            kv_remote(item, j).wait_recv()
        values_t[:HD, :] = values[item].T
        for c in range(2):
            here = (i == 0) & (core == 0)

            if c == 0:

                @pl.when(here)
                def _():
                    q_local.wait()

                @pl.when(jnp.logical_not(here))
                def _():
                    pltpu.make_async_remote_copy(
                        src_ref=own_q, dst_ref=queries.at[item, 0], send_sem=q_send.at[0, 0],
                        recv_sem=q_recv.at[item, 0], device_id=device(y, half, 1 - core, z, low),
                        device_id_type=MESH,
                    ).wait_recv()

            else:
                pltpu.make_async_remote_copy(
                    src_ref=own_q, dst_ref=queries.at[item, 1], send_sem=q_send.at[0, 0],
                    recv_sem=q_recv.at[item, 1], device_id=device(y, half, 1 - core, z, low),
                    device_id_type=MESH,
                ).wait_recv()
            q_rows = heads_in_rows(queries[item, c])
            scores = lax.dot_general(keys[item], q_rows, NT, preferred_element_type=F32)
            peak = jnp.max(scores, axis=0, keepdims=True)
            probs = jnp.exp2((scores - peak) * SCALE).astype(BF16)
            both = jnp.dot(values_t[...], probs, preferred_element_type=F32)
            parts[item, c] = both[:HD].astype(BF16)
            for k in range(HERE):
                part_stats[item, c, k : k + 1, :] = peak[:, k * LS : (k + 1) * LS]
                part_stats[item, c, HERE + k : HERE + k + 1, :] = both[
                    HD : HD + 1, k * LS : (k + 1) * LS
                ]
            if c == 0:

                @pl.when(jnp.logical_not(here))
                def _():
                    out_copy(item, 0).start()
                    stat_copy(item, 0).start()

                @pl.when(here)
                def _():
                    got[y * 2] = parts[item, 0]
                    got_stats[y * 2] = part_stats[item, 0]

            else:
                out_copy(item, 1).start()
                stat_copy(item, 1).start()
        return carry

    lax.fori_loop(0, NY, one_item, 0)

    for dy in (0, 1, 3, 2):
        for c in range(2):
            slot = ((y + dy) % NY) * 2 + c

            def wait_slot(slot=slot):
                for buffer, source, send, recv in (
                    (got, parts, o_send, o_recv),
                    (got_stats, part_stats, s_send, s_recv),
                ):
                    pltpu.make_async_remote_copy(
                        src_ref=source.at[0, 0], dst_ref=buffer.at[slot], send_sem=send.at[0, 0],
                        recv_sem=recv.at[slot], device_id=device(y, half, 1 - core, z, low),
                        device_id_type=MESH,
                    ).wait_recv()

            if (dy, c) == (0, 0):
                pl.when(core == 1)(wait_slot)
            else:
                wait_slot()

    live = lax.broadcasted_iota(jnp.int32, (LS, HD), 0) < len_ref[0]
    for k in range(HERE):
        lanes = slice(k * LS, (k + 1) * LS)
        own_peak = suffix_stats[k : k + 1, :]
        peaks = [got_stats[s, k : k + 1, :] for s in range(2 * NY)]
        highest = functools.reduce(jnp.maximum, peaks, own_peak)
        weight = jnp.exp2((own_peak - highest) * SCALE)
        over = suffix_sum[:, lanes] * weight
        under = suffix_stats[HERE + k : HERE + k + 1, :] * weight
        for s in range(2 * NY):
            weight = jnp.exp2((peaks[s] - highest) * SCALE)
            over = over + got[s, :, lanes].astype(F32) * weight
            under = under + got_stats[s, HERE + k : HERE + k + 1, :] * weight
        mixed = (over / under).T
        out_ref[:, k * HD : (k + 1) * HD] = jnp.where(live, mixed, 0.0).astype(BF16)

    @pl.when(core == 1)
    def _():
        q_copy(0, 0).wait_send()

    q_copy(0, 1).wait_send()
    for dy in (1, 3, 2):
        q_copy(dy, 0).wait_send()
        q_copy(dy, 1).wait_send()
    for i in range(NY):
        for j in range(2):
            kv_remote(order(i), j).wait_send()
        for c in range(2):

            def wait_sent(i=i, c=c):
                out_copy(order(i), c).wait_send()
                stat_copy(order(i), c).wait_send()

            if (i, c) == (0, 0):
                pl.when(core == 1)(wait_sent)
            else:
                wait_sent()


def on_device(queries, suffix_keys, suffix_values, prefix_keys, prefix_values, lengths):
    hbm = pl.BlockSpec(memory_space=pl.ANY)
    dma = pltpu.SemaphoreType.DMA
    out = pl.pallas_call(
        kernel,
        name="attend",
        out_shape=jax.ShapeDtypeStruct((LS, HERE * HD), BF16),
        in_specs=[hbm] * 5 + [pl.BlockSpec(memory_space=pltpu.SMEM)],
        out_specs=pl.BlockSpec(memory_space=pltpu.VMEM),
        scratch_shapes=[
            pltpu.VMEM((LS, HERE * HD), BF16),
            pltpu.VMEM((LS, HD), BF16),
            pltpu.VMEM((LS, HD), BF16),
            pltpu.VMEM((NY, 2 * P_DEV, HD), BF16),
            pltpu.VMEM((NY, 2 * P_DEV, HD), BF16),
            pltpu.VMEM((HD + ONES, 2 * P_DEV), BF16),
            pltpu.VMEM((NY, 2, LS, HERE * HD), BF16),
            pltpu.VMEM((NY, 2, HD, W), BF16),
            pltpu.VMEM((NY, 2, 2 * HERE, LS), F32),
            pltpu.VMEM((2 * NY, HD, W), BF16),
            pltpu.VMEM((2 * NY, 2 * HERE, LS), F32),
            pltpu.VMEM((HD, W), F32),
            pltpu.VMEM((2 * HERE, LS), F32),
            dma((3,)),
            dma((NY, 2)),
            dma((NY, 2)),
            dma((NY, 2)),
            dma,
            dma((NY, 2)),
            dma((NY, 2)),
            dma((NY, 2)),
            dma((2 * NY,)),
            dma((NY, 2)),
            dma((2 * NY,)),
        ],
        compiler_params=pltpu.CompilerParams(
            collective_id=0, has_side_effects=True, vmem_limit_bytes=62 * 2**20
        ),
        cost_estimate=pl.CostEstimate(
            flops=4 * 8192 * 1024 * 128, bytes_accessed=6 * 2**20, transcendentals=8192 * 1024
        ),
    )(
        queries.reshape(LS, HERE * HD),
        suffix_keys.reshape(LS, KVH * HD),
        suffix_values.reshape(LS, KVH * HD),
        prefix_keys,
        prefix_values,
        lengths,
    )
    return out.reshape(1, LS, HERE * HD)


def solution(mesh):
    in_specs = (
        P("cand", None, "ctx"),
        P("cand", None, None),
        P("cand", None, None),
        P("ctx", None),
        P("ctx", None),
        P("cand"),
    )
    return jax.shard_map(
        on_device, mesh=mesh, in_specs=in_specs, out_specs=P("cand", None, "ctx"), check_vma=False
    )
```

```python
import functools
import math

import jax
import jax.numpy as jnp
from jax import lax
from jax.experimental import pallas as pl
from jax.experimental.pallas import tpu as pltpu
from jax.sharding import PartitionSpec as P

H = 64
KVH = 8
HD = 128
LS = 128
P_DEV = 1024
NY = 4
HERE = 4
W = HERE * LS
TILES = 8
KEYS = 2 * P_DEV
CHUNK = 512
STEP = (0, -1, 2, 1, -1, 2, 0, 1)
SIDE = (0, 0, 0, 1, 1, 1, 1, 0)
SENT_TO = (0, 0, 0, 0, 0, 1, 1, 0)
MIRROR = (0, 7, 2, 4, 3, 5, 6, 1)
ONES = 8


MESH = pl.DeviceIdType.MESH
NT = (((1,), (1,)), ((), ()))
TN = (((0,), (0,)), ((), ()))
SCALE = math.log2(math.e) / math.sqrt(HD)
F32 = jnp.float32
BF16 = jnp.bfloat16


def place():
    ctx, cand = lax.axis_index("ctx"), lax.axis_index("cand")
    return ctx // 4, (ctx // 2) % 2, ctx % 2, cand // 2, cand % 2


def heads_in_rows(block):
    return jnp.concatenate([block[:, i * HD : (i + 1) * HD] for i in range(HERE)], axis=0)


def kernel(
    q_hbm, sk_hbm, sv_hbm, pk_hbm, pv_hbm, len_ref, out_ref,
    own_q, suffix_k, suffix_v, keys, values, values_t, queries, scores, probs, parts, part_stats, got, got_stats,
    total, stats,
    own_sem, kv_sem, kv_send, kv_recv, q_send, q_recv, o_send, o_recv, s_send, s_recv,
):
    y, half, core, z, low = place()

    onward = 1 - 2 * core

    def device(step, other, c):
        return {
            "ctx": (((y + NY + step * onward) % NY) * 2 + (half + other) % 2) * 2 + c,
            "cand": z * 2 + (low + other) % 2,
        }

    def pick(table, t):
        if isinstance(t, int):
            return table[t]
        return functools.reduce(lambda x, k: jnp.where(t == k, table[k], x), range(1, TILES), table[0])

    def remote(src, dst, send, recv, target):
        return pltpu.make_async_remote_copy(
            src_ref=src, dst_ref=dst, send_sem=send, recv_sem=recv, device_id=target, device_id_type=MESH
        )

    columns = pl.ds(pl.multiple_of((y * 2 + half) * HD, HD), HD)
    own_copies = [
        pltpu.make_async_copy(q_hbm, own_q, own_sem.at[0]),
        pltpu.make_async_copy(sk_hbm.at[:, columns], suffix_k, own_sem.at[1]),
        pltpu.make_async_copy(sv_hbm.at[:, columns], suffix_v, own_sem.at[2]),
    ]
    own, other_core = slice(0, P_DEV), slice(P_DEV, KEYS)

    def kv_local(t, j):
        kv_head = ((y + NY + STEP[t] * onward) % NY) * 2 + (half + SIDE[t]) % 2
        cols = pl.ds(pl.multiple_of(kv_head * HD, HD), HD)
        src, dst = ((pk_hbm, keys), (pv_hbm, values))[j]
        return pltpu.make_async_copy(src.at[:, cols], dst.at[t, own, :], kv_sem.at[t, j])

    def kv_remote(t, j):
        ref = (keys, values)[j]
        return remote(
            ref.at[pick(MIRROR, t), own, :], ref.at[t, other_core, :], kv_send.at[t, j], kv_recv.at[t, j],
            device(0, 0, 1 - core),
        )

    barrier = pltpu.get_barrier_semaphore()
    for dy, other, c in ((0, 0, 1 - core), (0, 1, core), (1, 0, core), (-1, 0, core)):
        pl.semaphore_signal(barrier, inc=1, device_id=device(dy, other, c), device_id_type=MESH)

    for j in range(2):
        kv_local(0, j).start()
    for copy in own_copies:
        copy.start()
    for t in (1, 7):
        for j in range(2):
            kv_local(t, j).start()
    pl.semaphore_wait(barrier, 4)

    def q_copy(src, n, slot, step, other):
        return remote(src, queries.at[slot], q_send.at[n], q_recv.at[slot], device(step, other, core))

    q_copies = [
        q_copy(q_hbm, 0, 1, 1, 0),
        q_copy(q_hbm, 1, 6, 0, 1),
        q_copy(q_hbm, 2, 7, -1, 0),
        q_copy(queries.at[1], 3, 2, 1, 0),
        q_copy(queries.at[1], 4, 4, 0, 1),
        q_copy(queries.at[6], 5, 3, -1, 0),
        q_copy(queries.at[2], 6, 5, 0, 1),
    ]

    def q_arrived(t):
        remote(own_q, queries.at[t], q_send.at[0], q_recv.at[t], device(0, 0, 1 - core)).wait_recv()

    def kv_arrived(t):
        for j in range(2):
            kv_remote(t, j).wait_recv()

    def kv_out(t):
        for j in range(2):
            if t <= MIRROR[t]:
                for m in sorted({t, MIRROR[t]}):
                    kv_local(m, j).wait()
            kv_remote(t, j).start()

    q_copies[0].start()
    q_copies[1].start()
    kv_out(0)
    for t in range(2, 7):
        for j in range(2):
            kv_local(t, j).start()
    kv_out(1)

    for copy in own_copies:
        copy.wait()
    q_rows = heads_in_rows(own_q[...])
    s = lax.dot_general(suffix_k[...], q_rows, NT, preferred_element_type=F32)
    u = lax.broadcasted_iota(jnp.int32, (LS, W), 0)
    t = lax.broadcasted_iota(jnp.int32, (LS, W), 1) % LS
    s = jnp.where(u <= t, s, -1e30)
    peak = jnp.max(s, axis=0, keepdims=True)
    p = jnp.exp2((s - peak) * SCALE)
    under = jnp.sum(p, axis=0, keepdims=True)
    total[...] = lax.dot_general(suffix_v[...], p.astype(BF16), TN, preferred_element_type=F32)
    for i in range(HERE):
        stats[i : i + 1, :] = peak[:, i * LS : (i + 1) * LS]
        stats[HERE + i : HERE + i + 1, :] = under[:, i * LS : (i + 1) * LS]

    q_copies[0].wait_send()
    q_copies[2].start()

    for i in range(2):
        values_t[i, HD:, :] = jnp.ones((ONES, KEYS), BF16)
    queries[0] = own_q[...]

    def out_copies(t):
        target = device(pick(STEP, t), pick(SENT_TO, t), core)
        return [
            remote(parts.at[t], got.at[t], o_send.at[t], o_recv.at[t], target),
            remote(part_stats.at[t], got_stats.at[t], s_send.at[t], s_recv.at[t], target),
        ]

    def finish(t, peak, sums, lanes):
        parts[t, :, lanes] = sums[:HD].astype(BF16)
        for k in range(lanes.start // LS, lanes.stop // LS):
            at = slice(k * LS, (k + 1) * LS)
            part_stats[t, k : k + 1, :] = peak[:, at]
            part_stats[t, HERE + k : HERE + k + 1, :] = sums[
                HD : HD + 1, k * LS - lanes.start : (k + 1) * LS - lanes.start
            ]

    def score(i, t, q_rows, at):
        s = lax.dot_general(keys[t, at, :], q_rows, NT, preferred_element_type=F32)
        scores[i, at, :] = s
        return jnp.max(s, axis=0, keepdims=True)

    def soften(i, peak, at):
        probs[i, at, :] = jnp.exp2((scores[i, at, :] - peak) * SCALE).astype(BF16)

    chunks = [slice(k, k + CHUNK) for k in range(0, KEYS, CHUNK)]

    def pair(i, carry):
        a, b = 2 * i, 2 * i + 1
        kv_arrived(a)

        @pl.when(i == 0)
        def _():
            kv_out(2)
            kv_out(3)

        @pl.when(i == 1)
        def _():
            kv_out(6)
            kv_out(7)
            q_arrived(2)
            q_copies[6].start()

        @pl.when(i == 2)
        def _():
            q_arrived(4)

        q_rows = heads_in_rows(queries[a])
        peak = functools.reduce(jnp.maximum, [score(0, a, q_rows, at) for at in chunks])
        values_t[0, :HD, :] = values[a].T
        kv_arrived(b)

        @pl.when(i == 0)
        def _():
            q_arrived(1)
            q_copies[3].start()
            q_copies[4].start()
            kv_out(4)
            kv_out(5)

        @pl.when(i == 1)
        def _():
            q_arrived(3)

        @pl.when(i == 2)
        def _():
            q_arrived(5)

        @pl.when(i == 3)
        def _():
            q_arrived(7)

        q_rows = heads_in_rows(queries[b])
        peak_b = []
        for at in chunks:
            peak_b.append(score(1, b, q_rows, at))
            soften(0, peak, at)
        peak_b = functools.reduce(jnp.maximum, peak_b)
        values_t[1, :HD, :] = values[b].T

        @pl.when(i == 0)
        def _():
            q_arrived(6)
            q_copies[5].start()

        for n in range(2):
            lanes = slice(n * W // 2, (n + 1) * W // 2)
            sums = jnp.dot(values_t[0], probs[0, :, lanes], preferred_element_type=F32)
            finish(a, peak, sums, lanes)
            for at in chunks[2 * n : 2 * n + 2]:
                soften(1, peak_b, at)

        @pl.when((i == 1) | (i == 2))
        def _():
            for copy in out_copies(a):
                copy.start()

        sums = jnp.dot(values_t[1], probs[1], preferred_element_type=F32)
        finish(b, peak_b, sums, slice(0, W))
        for copy in out_copies(b):
            copy.start()

        return carry

    lax.fori_loop(0, TILES // 2, pair, 0)

    def add(pieces, k):
        lanes = slice(k * LS, (k + 1) * LS)
        peaks = [at[k : k + 1, :] for _, at in pieces]
        highest = functools.reduce(jnp.maximum, peaks)
        over, under = 0.0, 0.0
        for (part, at), peak in zip(pieces, peaks, strict=True):
            weight = jnp.exp2((peak - highest) * SCALE)
            over = over + part[:, lanes].astype(F32) * weight
            under = under + at[HERE + k : HERE + k + 1, :] * weight
        return over, under, highest

    def fold(pieces, part, at):
        for k in range(HERE):
            over, under, highest = add(pieces, k)
            part[:, k * LS : (k + 1) * LS] = over.astype(part.dtype)
            at[k : k + 1, :] = highest
            at[HERE + k : HERE + k + 1, :] = under

    def arrived(ts):
        for t in ts:
            for copy in out_copies(t):
                copy.wait_recv()
        return [(got.at[t], got_stats.at[t]) for t in ts]

    near = parts.at[6], part_stats.at[6]
    fold([near] + arrived((3, 4)), *near)
    for copy in out_copies(6):
        copy.start()
    so_far = total, stats
    fold([so_far, (parts.at[0], part_stats.at[0])] + arrived((1, 2)), *so_far)
    pieces = [so_far] + arrived((7, 5, 6))
    live = lax.broadcasted_iota(jnp.int32, (LS, HD), 0) < len_ref[0]
    for k in range(HERE):
        over, under, _ = add(pieces, k)
        mixed = (over * (1.0 / under)).T
        out_ref[:, k * HD : (k + 1) * HD] = jnp.where(live, mixed, 0.0).astype(BF16)

    for copy in q_copies[1:]:
        copy.wait_send()
    for t in range(TILES):
        for j in range(2):
            kv_remote(t, j).wait_send()
        if t > 0:
            for copy in out_copies(t):
                copy.wait_send()


def on_device(queries, suffix_keys, suffix_values, prefix_keys, prefix_values, lengths):
    hbm = pl.BlockSpec(memory_space=pl.ANY)
    dma = pltpu.SemaphoreType.DMA
    out = pl.pallas_call(
        kernel,
        name="attend",
        out_shape=jax.ShapeDtypeStruct((LS, HERE * HD), BF16),
        in_specs=[hbm] * 5 + [pl.BlockSpec(memory_space=pltpu.SMEM)],
        out_specs=pl.BlockSpec(memory_space=pltpu.VMEM),
        scratch_shapes=[
            pltpu.VMEM((LS, HERE * HD), BF16),
            pltpu.VMEM((LS, HD), BF16),
            pltpu.VMEM((LS, HD), BF16),
            pltpu.VMEM((TILES, KEYS, HD), BF16),
            pltpu.VMEM((TILES, KEYS, HD), BF16),
            pltpu.VMEM((2, HD + ONES, KEYS), BF16),
            pltpu.VMEM((TILES, LS, HERE * HD), BF16),
            pltpu.VMEM((2, KEYS, W), F32),
            pltpu.VMEM((2, KEYS, W), BF16),
            pltpu.VMEM((TILES, HD, W), BF16),
            pltpu.VMEM((TILES, 2 * HERE, LS), F32),
            pltpu.VMEM((TILES, HD, W), BF16),
            pltpu.VMEM((TILES, 2 * HERE, LS), F32),
            pltpu.VMEM((HD, W), F32),
            pltpu.VMEM((2 * HERE, LS), F32),
            dma((3,)),
            dma((TILES, 2)),
            dma((TILES, 2)),
            dma((TILES, 2)),
            dma((7,)),
            dma((TILES,)),
            dma((TILES,)),
            dma((TILES,)),
            dma((TILES,)),
            dma((TILES,)),
        ],
        compiler_params=pltpu.CompilerParams(
            collective_id=0, has_side_effects=True, vmem_limit_bytes=62 * 2**20
        ),
        cost_estimate=pl.CostEstimate(
            flops=4 * 8192 * 1024 * 128, bytes_accessed=6 * 2**20, transcendentals=8192 * 1024
        ),
    )(
        queries.reshape(LS, HERE * HD),
        suffix_keys.reshape(LS, KVH * HD),
        suffix_values.reshape(LS, KVH * HD),
        prefix_keys,
        prefix_values,
        lengths,
    )
    return out.reshape(1, LS, HERE * HD)


def solution(mesh):
    in_specs = (
        P("cand", None, "ctx"),
        P("cand", None, None),
        P("cand", None, None),
        P("ctx", None),
        P("ctx", None),
        P("cand"),
    )
    return jax.shard_map(
        on_device, mesh=mesh, in_specs=in_specs, out_specs=P("cand", None, "ctx"), check_vma=False
    )
```

```python
import functools
import math

import jax
import jax.numpy as jnp
from jax import lax
from jax.experimental import pallas as pl
from jax.experimental.pallas import tpu as pltpu
from jax.sharding import PartitionSpec as P

H = 64
KVH = 8
HD = 128
LS = 128
P_DEV = 1024
NY = 4
HERE = 4
W = HERE * LS
TILES = 8
KEYS = 2 * P_DEV
CHUNK = 512
STEP = (0, -1, 2, 1, -1, 2, 0, 1)
SIDE = (0, 0, 0, 1, 1, 1, 1, 0)
SENT_TO = (0, 0, 0, 0, 0, 1, 1, 0)
MIRROR = (0, 7, 2, 4, 3, 5, 6, 1)
ONES = 8


MESH = pl.DeviceIdType.MESH
NT = (((1,), (1,)), ((), ()))
TN = (((0,), (0,)), ((), ()))
SCALE = math.log2(math.e) / math.sqrt(HD)
F32 = jnp.float32
BF16 = jnp.bfloat16


def place():
    ctx, cand = lax.axis_index("ctx"), lax.axis_index("cand")
    return ctx // 4, (ctx // 2) % 2, ctx % 2, cand // 2, cand % 2


def heads_in_rows(block):
    return jnp.concatenate([block[:, i * HD : (i + 1) * HD] for i in range(HERE)], axis=0)


def kernel(
    q_hbm, sk_hbm, sv_hbm, pk_hbm, pv_hbm, len_ref, out_ref,
    own_q, suffix_k, suffix_v, keys, values, values_t, queries, scores, probs, parts, part_stats, got, got_stats,
    total, stats,
    own_sem, kv_sem, kv_send, kv_recv, q_send, q_recv, o_send, o_recv, s_send, s_recv,
):
    y, half, core, z, low = place()

    onward = 1 - 2 * core

    def device(step, other, c):
        return {
            "ctx": (((y + NY + step * onward) % NY) * 2 + (half + other) % 2) * 2 + c,
            "cand": z * 2 + (low + other) % 2,
        }

    def pick(table, t):
        if isinstance(t, int):
            return table[t]
        return functools.reduce(lambda x, k: jnp.where(t == k, table[k], x), range(1, TILES), table[0])

    def remote(src, dst, send, recv, target):
        return pltpu.make_async_remote_copy(
            src_ref=src, dst_ref=dst, send_sem=send, recv_sem=recv, device_id=target, device_id_type=MESH
        )

    columns = pl.ds(pl.multiple_of((y * 2 + half) * HD, HD), HD)
    own_copies = [
        pltpu.make_async_copy(q_hbm, own_q, own_sem.at[0]),
        pltpu.make_async_copy(sk_hbm.at[:, columns], suffix_k, own_sem.at[1]),
        pltpu.make_async_copy(sv_hbm.at[:, columns], suffix_v, own_sem.at[2]),
    ]
    own, other_core = slice(0, P_DEV), slice(P_DEV, KEYS)

    def kv_local(t, j):
        kv_head = ((y + NY + STEP[t] * onward) % NY) * 2 + (half + SIDE[t]) % 2
        cols = pl.ds(pl.multiple_of(kv_head * HD, HD), HD)
        src, dst = ((pk_hbm, keys), (pv_hbm, values))[j]
        return pltpu.make_async_copy(src.at[:, cols], dst.at[t, own, :], kv_sem.at[t, j])

    def kv_remote(t, j):
        ref = (keys, values)[j]
        return remote(
            ref.at[pick(MIRROR, t), own, :], ref.at[t, other_core, :], kv_send.at[t, j], kv_recv.at[t, j],
            device(0, 0, 1 - core),
        )

    barrier = pltpu.get_barrier_semaphore()
    for dy, other, c in ((0, 0, 1 - core), (0, 1, core), (1, 0, core), (-1, 0, core)):
        pl.semaphore_signal(barrier, inc=1, device_id=device(dy, other, c), device_id_type=MESH)

    for j in range(2):
        kv_local(0, j).start()
    for copy in own_copies:
        copy.start()
    for t in (1, 7):
        for j in range(2):
            kv_local(t, j).start()
    pl.semaphore_wait(barrier, 4)

    def q_copy(src, n, slot, step, other):
        return remote(src, queries.at[slot], q_send.at[n], q_recv.at[slot], device(step, other, core))

    q_copies = [
        q_copy(q_hbm, 0, 1, 1, 0),
        q_copy(q_hbm, 1, 6, 0, 1),
        q_copy(q_hbm, 2, 7, -1, 0),
        q_copy(queries.at[1], 3, 2, 1, 0),
        q_copy(queries.at[1], 4, 4, 0, 1),
        q_copy(queries.at[6], 5, 3, -1, 0),
        q_copy(queries.at[2], 6, 5, 0, 1),
    ]

    def q_arrived(t):
        remote(own_q, queries.at[t], q_send.at[0], q_recv.at[t], device(0, 0, 1 - core)).wait_recv()

    def kv_arrived(t):
        for j in range(2):
            kv_remote(t, j).wait_recv()

    def kv_out(t):
        for j in range(2):
            if t <= MIRROR[t]:
                for m in sorted({t, MIRROR[t]}):
                    kv_local(m, j).wait()
            kv_remote(t, j).start()

    q_copies[0].start()
    q_copies[1].start()
    kv_out(0)
    for t in range(2, 7):
        for j in range(2):
            kv_local(t, j).start()
    kv_out(1)

    for copy in own_copies:
        copy.wait()
    q_rows = heads_in_rows(own_q[...])
    s = lax.dot_general(suffix_k[...], q_rows, NT, preferred_element_type=F32)
    u = lax.broadcasted_iota(jnp.int32, (LS, W), 0)
    t = lax.broadcasted_iota(jnp.int32, (LS, W), 1) % LS
    s = jnp.where(u <= t, s, -1e30)
    peak = jnp.max(s, axis=0, keepdims=True)
    p = jnp.exp2((s - peak) * SCALE)
    under = jnp.sum(p, axis=0, keepdims=True)
    total[...] = lax.dot_general(suffix_v[...], p.astype(BF16), TN, preferred_element_type=F32)
    for i in range(HERE):
        stats[i : i + 1, :] = peak[:, i * LS : (i + 1) * LS]
        stats[HERE + i : HERE + i + 1, :] = under[:, i * LS : (i + 1) * LS]

    q_copies[0].wait_send()
    q_copies[2].start()

    values_t[HD:, :] = jnp.ones((ONES, KEYS), BF16)
    queries[0] = own_q[...]

    def out_copies(t):
        target = device(pick(STEP, t), pick(SENT_TO, t), core)
        return [
            remote(parts.at[t], got.at[t], o_send.at[t], o_recv.at[t], target),
            remote(part_stats.at[t], got_stats.at[t], s_send.at[t], s_recv.at[t], target),
        ]

    chunks = [slice(k, k + CHUNK) for k in range(0, KEYS, CHUNK)]
    halves = [slice(0, W // 2), slice(W // 2, W)]

    def tile(t, carry):
        kv_arrived(t)

        @pl.when(t == 0)
        def _():
            kv_out(2)
            kv_out(3)

        @pl.when(t == 1)
        def _():
            kv_out(4)
            kv_out(5)

        @pl.when(t == 2)
        def _():
            q_arrived(2)
            q_copies[6].start()
            kv_out(6)
            kv_out(7)

        @pl.when((t == 3) | (t == 4) | (t == 5) | (t == 7))
        def _():
            q_arrived(t)

        q_rows = heads_in_rows(queries[t])

        def score(n, at):
            s = lax.dot_general(keys[t, at, :], q_rows[halves[n]], NT, preferred_element_type=F32)
            scores[at, halves[n]] = s
            return jnp.max(s, axis=0, keepdims=True)

        def soften(n, peak, at):
            probs[at, halves[n]] = jnp.exp2((scores[at, halves[n]] - peak) * SCALE).astype(BF16)

        def finish(n, peak):
            sums = jnp.dot(values_t[...], probs[:, halves[n]], preferred_element_type=F32)
            parts[t, :, halves[n]] = sums[:HD].astype(BF16)
            for k in range(HERE // 2):
                at, head = slice(k * LS, (k + 1) * LS), n * HERE // 2 + k
                part_stats[t, head : head + 1, :] = peak[:, at]
                part_stats[t, HERE + head : HERE + head + 1, :] = sums[HD : HD + 1, at]

        peak = functools.reduce(jnp.maximum, [score(0, at) for at in chunks])
        values_t[:HD, :] = values[t].T
        next_peak = []
        for at in chunks:
            next_peak.append(score(1, at))
            soften(0, peak, at)
        next_peak = functools.reduce(jnp.maximum, next_peak)

        @pl.when(t == 0)
        def _():
            q_arrived(1)
            q_copies[3].start()
            q_copies[4].start()

        finish(0, peak)
        for at in chunks:
            soften(1, next_peak, at)
        finish(1, next_peak)

        @pl.when((t != 0) & (t != 6))
        def _():
            for copy in out_copies(t):
                copy.start()

        @pl.when(t == 1)
        def _():
            q_arrived(6)
            q_copies[5].start()

        return carry

    lax.fori_loop(0, TILES, tile, 0)

    def add(pieces, k):
        lanes = slice(k * LS, (k + 1) * LS)
        peaks = [at[k : k + 1, :] for _, at in pieces]
        highest = functools.reduce(jnp.maximum, peaks)
        over, under = 0.0, 0.0
        for (part, at), peak in zip(pieces, peaks, strict=True):
            weight = jnp.exp2((peak - highest) * SCALE)
            over = over + part[:, lanes].astype(F32) * weight
            under = under + at[HERE + k : HERE + k + 1, :] * weight
        return over, under, highest

    def fold(pieces, part, at):
        for k in range(HERE):
            over, under, highest = add(pieces, k)
            part[:, k * LS : (k + 1) * LS] = over.astype(part.dtype)
            at[k : k + 1, :] = highest
            at[HERE + k : HERE + k + 1, :] = under

    def arrived(ts):
        for t in ts:
            for copy in out_copies(t):
                copy.wait_recv()
        return [(got.at[t], got_stats.at[t]) for t in ts]

    near = parts.at[6], part_stats.at[6]
    fold([near] + arrived((3, 4)), *near)
    for copy in out_copies(6):
        copy.start()
    so_far = total, stats
    fold([so_far, (parts.at[0], part_stats.at[0])] + arrived((1, 2)), *so_far)
    pieces = [so_far] + arrived((7, 5, 6))
    live = lax.broadcasted_iota(jnp.int32, (LS, HD), 0) < len_ref[0]
    for k in range(HERE):
        over, under, _ = add(pieces, k)
        mixed = (over * (1.0 / under)).T
        out_ref[:, k * HD : (k + 1) * HD] = jnp.where(live, mixed, 0.0).astype(BF16)

    for copy in q_copies[1:]:
        copy.wait_send()
    for t in range(TILES):
        for j in range(2):
            kv_remote(t, j).wait_send()
        if t > 0:
            for copy in out_copies(t):
                copy.wait_send()


def on_device(queries, suffix_keys, suffix_values, prefix_keys, prefix_values, lengths):
    hbm = pl.BlockSpec(memory_space=pl.ANY)
    dma = pltpu.SemaphoreType.DMA
    out = pl.pallas_call(
        kernel,
        name="attend",
        out_shape=jax.ShapeDtypeStruct((LS, HERE * HD), BF16),
        in_specs=[hbm] * 5 + [pl.BlockSpec(memory_space=pltpu.SMEM)],
        out_specs=pl.BlockSpec(memory_space=pltpu.VMEM),
        scratch_shapes=[
            pltpu.VMEM((LS, HERE * HD), BF16),
            pltpu.VMEM((LS, HD), BF16),
            pltpu.VMEM((LS, HD), BF16),
            pltpu.VMEM((TILES, KEYS, HD), BF16),
            pltpu.VMEM((TILES, KEYS, HD), BF16),
            pltpu.VMEM((HD + ONES, KEYS), BF16),
            pltpu.VMEM((TILES, LS, HERE * HD), BF16),
            pltpu.VMEM((KEYS, W), F32),
            pltpu.VMEM((KEYS, W), BF16),
            pltpu.VMEM((TILES, HD, W), BF16),
            pltpu.VMEM((TILES, 2 * HERE, LS), F32),
            pltpu.VMEM((TILES, HD, W), BF16),
            pltpu.VMEM((TILES, 2 * HERE, LS), F32),
            pltpu.VMEM((HD, W), F32),
            pltpu.VMEM((2 * HERE, LS), F32),
            dma((3,)),
            dma((TILES, 2)),
            dma((TILES, 2)),
            dma((TILES, 2)),
            dma((7,)),
            dma((TILES,)),
            dma((TILES,)),
            dma((TILES,)),
            dma((TILES,)),
            dma((TILES,)),
        ],
        compiler_params=pltpu.CompilerParams(
            collective_id=0, has_side_effects=True, vmem_limit_bytes=62 * 2**20
        ),
        cost_estimate=pl.CostEstimate(
            flops=4 * 8192 * 1024 * 128, bytes_accessed=6 * 2**20, transcendentals=8192 * 1024
        ),
    )(
        queries.reshape(LS, HERE * HD),
        suffix_keys.reshape(LS, KVH * HD),
        suffix_values.reshape(LS, KVH * HD),
        prefix_keys,
        prefix_values,
        lengths,
    )
    return out.reshape(1, LS, HERE * HD)


def solution(mesh):
    in_specs = (
        P("cand", None, "ctx"),
        P("cand", None, None),
        P("cand", None, None),
        P("ctx", None),
        P("ctx", None),
        P("cand"),
    )
    return jax.shard_map(
        on_device, mesh=mesh, in_specs=in_specs, out_specs=P("cand", None, "ctx"), check_vma=False
    )
```

```python
import functools
import math

import jax
import jax.numpy as jnp
from jax import lax
from jax.experimental import pallas as pl
from jax.experimental.pallas import tpu as pltpu
from jax.sharding import PartitionSpec as P

H = 64
KVH = 8
HD = 128
LS = 128
P_DEV = 1024
NY = 4
HERE = 4
W = HERE * LS
TILES = 8
KEYS = 2 * P_DEV
CHUNK = 512
STEP = (0, -1, 2, 1, -1, 2, 0, 1)
SIDE = (0, 0, 0, 1, 1, 1, 1, 0)
SENT_TO = (0, 0, 0, 0, 0, 1, 1, 0)
MIRROR = (0, 7, 2, 4, 3, 5, 6, 1)
ONES = 8


MESH = pl.DeviceIdType.MESH
NT = (((1,), (1,)), ((), ()))
TN = (((0,), (0,)), ((), ()))
SCALE = math.log2(math.e) / math.sqrt(HD)
F32 = jnp.float32
BF16 = jnp.bfloat16


def place():
    ctx, cand = lax.axis_index("ctx"), lax.axis_index("cand")
    return ctx // 4, (ctx // 2) % 2, ctx % 2, cand // 2, cand % 2


def heads_in_rows(block):
    return jnp.concatenate([block[:, i * HD : (i + 1) * HD] for i in range(HERE)], axis=0)


def kernel(
    q_hbm, sk_hbm, sv_hbm, pk_hbm, pv_hbm, len_ref, out_ref,
    own_q, suffix_k, suffix_v, keys, values, values_t, queries, scores, probs, parts, part_stats, got, got_stats,
    total, stats,
    own_sem, kv_sem, kv_send, kv_recv, q_send, q_recv, o_send, o_recv, s_send, s_recv,
):
    y, half, core, z, low = place()

    onward = 1 - 2 * core

    def device(step, other, c):
        return {
            "ctx": (((y + NY + step * onward) % NY) * 2 + (half + other) % 2) * 2 + c,
            "cand": z * 2 + (low + other) % 2,
        }

    def pick(table, t):
        if isinstance(t, int):
            return table[t]
        return functools.reduce(lambda x, k: jnp.where(t == k, table[k], x), range(1, TILES), table[0])

    def remote(src, dst, send, recv, target):
        return pltpu.make_async_remote_copy(
            src_ref=src, dst_ref=dst, send_sem=send, recv_sem=recv, device_id=target, device_id_type=MESH
        )

    columns = pl.ds(pl.multiple_of((y * 2 + half) * HD, HD), HD)
    own_copies = [
        pltpu.make_async_copy(q_hbm, own_q, own_sem.at[0]),
        pltpu.make_async_copy(sk_hbm.at[:, columns], suffix_k, own_sem.at[1]),
        pltpu.make_async_copy(sv_hbm.at[:, columns], suffix_v, own_sem.at[2]),
    ]
    own, other_core = slice(0, P_DEV), slice(P_DEV, KEYS)

    def kv_local(t, j):
        kv_head = ((y + NY + STEP[t] * onward) % NY) * 2 + (half + SIDE[t]) % 2
        cols = pl.ds(pl.multiple_of(kv_head * HD, HD), HD)
        src, dst = ((pk_hbm, keys), (pv_hbm, values))[j]
        return pltpu.make_async_copy(src.at[:, cols], dst.at[t, own, :], kv_sem.at[t, j])

    def kv_remote(t, j):
        ref = (keys, values)[j]
        return remote(
            ref.at[pick(MIRROR, t), own, :], ref.at[t, other_core, :], kv_send.at[t, j], kv_recv.at[t, j],
            device(0, 0, 1 - core),
        )

    barrier = pltpu.get_barrier_semaphore()
    for dy, other, c in ((0, 0, 1 - core), (0, 1, core), (1, 0, core), (-1, 0, core)):
        pl.semaphore_signal(barrier, inc=1, device_id=device(dy, other, c), device_id_type=MESH)

    for j in range(2):
        kv_local(0, j).start()
    for copy in own_copies:
        copy.start()
    for t in (1, 7):
        for j in range(2):
            kv_local(t, j).start()
    pl.semaphore_wait(barrier, 4)

    def q_copy(src, n, slot, step, other):
        return remote(src, queries.at[slot], q_send.at[n], q_recv.at[slot], device(step, other, core))

    q_copies = [
        q_copy(q_hbm, 0, 1, 1, 0),
        q_copy(q_hbm, 1, 6, 0, 1),
        q_copy(q_hbm, 2, 7, -1, 0),
        q_copy(queries.at[1], 3, 2, 1, 0),
        q_copy(queries.at[1], 4, 4, 0, 1),
        q_copy(queries.at[6], 5, 3, -1, 0),
        q_copy(queries.at[2], 6, 5, 0, 1),
    ]

    def q_arrived(t):
        remote(own_q, queries.at[t], q_send.at[0], q_recv.at[t], device(0, 0, 1 - core)).wait_recv()

    def k_arrived(t):
        kv_remote(t, 0).wait_recv()

    def v_arrived(t):
        kv_remote(t, 1).wait_recv()

    def kv_out(t):
        for j in range(2):
            if t <= MIRROR[t]:
                for m in sorted({t, MIRROR[t]}):
                    kv_local(m, j).wait()
            kv_remote(t, j).start()

    q_copies[0].start()
    q_copies[1].start()
    kv_out(0)
    for t in range(2, 7):
        for j in range(2):
            kv_local(t, j).start()
    kv_out(1)

    for copy in own_copies:
        copy.wait()
    q_rows = heads_in_rows(own_q[...])
    s = lax.dot_general(suffix_k[...], q_rows, NT, preferred_element_type=F32)
    u = lax.broadcasted_iota(jnp.int32, (LS, W), 0)
    t = lax.broadcasted_iota(jnp.int32, (LS, W), 1) % LS
    s = jnp.where(u <= t, s, -1e30)
    peak = jnp.max(s, axis=0, keepdims=True)
    p = jnp.exp2((s - peak) * SCALE)
    under = jnp.sum(p, axis=0, keepdims=True)
    total[...] = lax.dot_general(suffix_v[...], p.astype(BF16), TN, preferred_element_type=F32)
    for i in range(HERE):
        stats[i : i + 1, :] = peak[:, i * LS : (i + 1) * LS]
        stats[HERE + i : HERE + i + 1, :] = under[:, i * LS : (i + 1) * LS]

    q_copies[0].wait_send()
    q_copies[2].start()

    values_t[HD:, :] = jnp.ones((ONES, KEYS), BF16)
    queries[0] = own_q[...]

    def out_copies(t):
        target = device(pick(STEP, t), pick(SENT_TO, t), core)
        return [
            remote(parts.at[t], got.at[t], o_send.at[t], o_recv.at[t], target),
            remote(part_stats.at[t], got_stats.at[t], s_send.at[t], s_recv.at[t], target),
        ]

    def add(pieces, k):
        lanes = slice(k * LS, (k + 1) * LS)
        peaks = [at[k : k + 1, :] for _, at in pieces]
        highest = functools.reduce(jnp.maximum, peaks)
        over, under = 0.0, 0.0
        for (part, at), peak in zip(pieces, peaks, strict=True):
            weight = jnp.exp2((peak - highest) * SCALE)
            over = over + part[:, lanes].astype(F32) * weight
            under = under + at[HERE + k : HERE + k + 1, :] * weight
        return over, under, highest

    def fold(pieces, part, at):
        for k in range(HERE):
            over, under, highest = add(pieces, k)
            part[:, k * LS : (k + 1) * LS] = over.astype(part.dtype)
            at[k : k + 1, :] = highest
            at[HERE + k : HERE + k + 1, :] = under

    def arrived(ts):
        for t in ts:
            for copy in out_copies(t):
                copy.wait_recv()
        return [(got.at[t], got_stats.at[t]) for t in ts]

    chunks = [slice(k, k + CHUNK) for k in range(0, KEYS, CHUNK)]
    halves = [slice(0, W // 2), slice(W // 2, W)]

    def tile(t, carry):
        k_arrived(t)

        @pl.when(t == 0)
        def _():
            kv_out(2)
            kv_out(3)
            q_arrived(1)
            q_copies[3].start()
            q_copies[4].start()

        @pl.when(t == 1)
        def _():
            kv_out(4)
            kv_out(5)

        @pl.when(t == 2)
        def _():
            q_arrived(2)
            q_copies[6].start()
            kv_out(6)
            kv_out(7)

        @pl.when((t == 3) | (t == 4) | (t == 5) | (t == 7))
        def _():
            q_arrived(t)

        q_rows = heads_in_rows(queries[t])

        def score(n, at):
            s = lax.dot_general(keys[t, at, :], q_rows[halves[n]], NT, preferred_element_type=F32)
            scores[at, halves[n]] = s
            return jnp.max(s, axis=0, keepdims=True)

        def soften(n, peak, at):
            probs[at, halves[n]] = jnp.exp2((scores[at, halves[n]] - peak) * SCALE).astype(BF16)

        def finish(n, peak):
            sums = jnp.dot(values_t[...], probs[:, halves[n]], preferred_element_type=F32)
            parts[t, :, halves[n]] = sums[:HD].astype(BF16)
            for k in range(HERE // 2):
                at, head = slice(k * LS, (k + 1) * LS), n * HERE // 2 + k
                part_stats[t, head : head + 1, :] = peak[:, at]
                part_stats[t, HERE + head : HERE + head + 1, :] = sums[HD : HD + 1, at]

        peak = functools.reduce(jnp.maximum, [score(0, at) for at in chunks])
        v_arrived(t)
        values_t[:HD, :] = values[t].T
        next_peak = []
        for at in chunks:
            next_peak.append(score(1, at))
            soften(0, peak, at)
        next_peak = functools.reduce(jnp.maximum, next_peak)

        @pl.when(t == 7)
        def _():
            near = parts.at[6], part_stats.at[6]
            fold([near] + arrived((3, 4)), *near)
            for copy in out_copies(6):
                copy.start()

        finish(0, peak)
        for at in chunks:
            soften(1, next_peak, at)
        finish(1, next_peak)

        @pl.when((t != 0) & (t != 6))
        def _():
            for copy in out_copies(t):
                copy.start()

        @pl.when(t == 0)
        def _():
            q_arrived(6)
            q_copies[5].start()

        return carry

    lax.fori_loop(0, TILES, tile, 0)

    so_far = total, stats
    fold([so_far, (parts.at[0], part_stats.at[0])] + arrived((1, 2)), *so_far)
    pieces = [so_far] + arrived((7, 5, 6))
    live = lax.broadcasted_iota(jnp.int32, (LS, HD), 0) < len_ref[0]
    for k in range(HERE):
        over, under, _ = add(pieces, k)
        mixed = (over * (1.0 / under)).T
        out_ref[:, k * HD : (k + 1) * HD] = jnp.where(live, mixed, 0.0).astype(BF16)

    for copy in q_copies[1:]:
        copy.wait_send()
    for t in range(TILES):
        for j in range(2):
            kv_remote(t, j).wait_send()
        if t > 0:
            for copy in out_copies(t):
                copy.wait_send()


def on_device(queries, suffix_keys, suffix_values, prefix_keys, prefix_values, lengths):
    hbm = pl.BlockSpec(memory_space=pl.ANY)
    dma = pltpu.SemaphoreType.DMA
    out = pl.pallas_call(
        kernel,
        name="attend",
        out_shape=jax.ShapeDtypeStruct((LS, HERE * HD), BF16),
        in_specs=[hbm] * 5 + [pl.BlockSpec(memory_space=pltpu.SMEM)],
        out_specs=pl.BlockSpec(memory_space=pltpu.VMEM),
        scratch_shapes=[
            pltpu.VMEM((LS, HERE * HD), BF16),
            pltpu.VMEM((LS, HD), BF16),
            pltpu.VMEM((LS, HD), BF16),
            pltpu.VMEM((TILES, KEYS, HD), BF16),
            pltpu.VMEM((TILES, KEYS, HD), BF16),
            pltpu.VMEM((HD + ONES, KEYS), BF16),
            pltpu.VMEM((TILES, LS, HERE * HD), BF16),
            pltpu.VMEM((KEYS, W), F32),
            pltpu.VMEM((KEYS, W), BF16),
            pltpu.VMEM((TILES, HD, W), BF16),
            pltpu.VMEM((TILES, 2 * HERE, LS), F32),
            pltpu.VMEM((TILES, HD, W), BF16),
            pltpu.VMEM((TILES, 2 * HERE, LS), F32),
            pltpu.VMEM((HD, W), F32),
            pltpu.VMEM((2 * HERE, LS), F32),
            dma((3,)),
            dma((TILES, 2)),
            dma((TILES, 2)),
            dma((TILES, 2)),
            dma((7,)),
            dma((TILES,)),
            dma((TILES,)),
            dma((TILES,)),
            dma((TILES,)),
            dma((TILES,)),
        ],
        compiler_params=pltpu.CompilerParams(
            collective_id=0, has_side_effects=True, vmem_limit_bytes=62 * 2**20
        ),
        cost_estimate=pl.CostEstimate(
            flops=4 * 8192 * 1024 * 128, bytes_accessed=6 * 2**20, transcendentals=8192 * 1024
        ),
    )(
        queries.reshape(LS, HERE * HD),
        suffix_keys.reshape(LS, KVH * HD),
        suffix_values.reshape(LS, KVH * HD),
        prefix_keys,
        prefix_values,
        lengths,
    )
    return out.reshape(1, LS, HERE * HD)


def solution(mesh):
    in_specs = (
        P("cand", None, "ctx"),
        P("cand", None, None),
        P("cand", None, None),
        P("ctx", None),
        P("ctx", None),
        P("cand"),
    )
    return jax.shard_map(
        on_device, mesh=mesh, in_specs=in_specs, out_specs=P("cand", None, "ctx"), check_vma=False
    )
```

```python
import functools
import math

import jax
import jax.numpy as jnp
from jax import lax
from jax.experimental import pallas as pl
from jax.experimental.pallas import tpu as pltpu
from jax.sharding import PartitionSpec as P

H = 64
KVH = 8
HD = 128
LS = 128
P_DEV = 1024
NY = 4
HERE = 4
W = HERE * LS
TILES = 8
KEYS = 2 * P_DEV
CHUNK = 512
STEP = (0, -1, 2, 1, -1, 2, 0, 1)
SIDE = (0, 0, 0, 1, 1, 1, 1, 0)
SENT_TO = (0, 0, 0, 0, 0, 1, 1, 0)
MIRROR = (0, 7, 2, 4, 3, 5, 6, 1)
ONES = 16


MESH = pl.DeviceIdType.MESH
NT = (((1,), (1,)), ((), ()))
TN = (((0,), (0,)), ((), ()))
SCALE = math.log2(math.e) / math.sqrt(HD)
F32 = jnp.float32
BF16 = jnp.bfloat16


def place():
    ctx, cand = lax.axis_index("ctx"), lax.axis_index("cand")
    return ctx // 4, (ctx // 2) % 2, ctx % 2, cand // 2, cand % 2


def heads_in_rows(block):
    return jnp.concatenate([block[:, i * HD : (i + 1) * HD] for i in range(HERE)], axis=0)


def kernel(
    q_hbm, sk_hbm, sv_hbm, pk_hbm, pv_hbm, len_ref, out_ref,
    own_q, suffix_k, suffix_v, keys, values, values_t, queries, scores, probs, parts, part_stats, got, got_stats,
    total, stats,
    own_sem, kv_sem, kv_send, kv_recv, q_send, q_recv, o_send, o_recv, s_send, s_recv,
):
    y, half, core, z, low = place()

    onward = 1 - 2 * core

    def device(step, other, c):
        return {
            "ctx": (((y + NY + step * onward) % NY) * 2 + (half + other) % 2) * 2 + c,
            "cand": z * 2 + (low + other) % 2,
        }

    def pick(table, t):
        if isinstance(t, int):
            return table[t]
        return functools.reduce(lambda x, k: jnp.where(t == k, table[k], x), range(1, TILES), table[0])

    def remote(src, dst, send, recv, target):
        return pltpu.make_async_remote_copy(
            src_ref=src, dst_ref=dst, send_sem=send, recv_sem=recv, device_id=target, device_id_type=MESH
        )

    columns = pl.ds(pl.multiple_of((y * 2 + half) * HD, HD), HD)
    own_copies = [
        pltpu.make_async_copy(q_hbm, own_q, own_sem.at[0]),
        pltpu.make_async_copy(sk_hbm.at[:, columns], suffix_k, own_sem.at[1]),
        pltpu.make_async_copy(sv_hbm.at[:, columns], suffix_v, own_sem.at[2]),
    ]
    own, other_core = slice(0, P_DEV), slice(P_DEV, KEYS)

    def kv_local(t, j):
        kv_head = ((y + NY + STEP[t] * onward) % NY) * 2 + (half + SIDE[t]) % 2
        cols = pl.ds(pl.multiple_of(kv_head * HD, HD), HD)
        src, dst = ((pk_hbm, keys), (pv_hbm, values))[j]
        return pltpu.make_async_copy(src.at[:, cols], dst.at[t, own, :], kv_sem.at[t, j])

    def kv_remote(t, j):
        ref = (keys, values)[j]
        return remote(
            ref.at[pick(MIRROR, t), own, :], ref.at[t, other_core, :], kv_send.at[t, j], kv_recv.at[t, j],
            device(0, 0, 1 - core),
        )

    barrier = pltpu.get_barrier_semaphore()
    for dy, other, c in ((0, 0, 1 - core), (0, 1, core), (1, 0, core), (-1, 0, core)):
        pl.semaphore_signal(barrier, inc=1, device_id=device(dy, other, c), device_id_type=MESH)

    for j in range(2):
        kv_local(0, j).start()
    for copy in own_copies:
        copy.start()
    for t in (1, 7):
        for j in range(2):
            kv_local(t, j).start()
    pl.semaphore_wait(barrier, 4)

    def q_copy(src, n, slot, step, other):
        return remote(src, queries.at[slot], q_send.at[n], q_recv.at[slot], device(step, other, core))

    q_copies = [
        q_copy(q_hbm, 0, 1, 1, 0),
        q_copy(q_hbm, 1, 6, 0, 1),
        q_copy(q_hbm, 2, 7, -1, 0),
        q_copy(queries.at[1], 3, 2, 1, 0),
        q_copy(queries.at[1], 4, 4, 0, 1),
        q_copy(queries.at[6], 5, 3, -1, 0),
        q_copy(queries.at[2], 6, 5, 0, 1),
    ]

    def q_arrived(t):
        remote(own_q, queries.at[t], q_send.at[0], q_recv.at[t], device(0, 0, 1 - core)).wait_recv()

    def k_arrived(t):
        kv_remote(t, 0).wait_recv()

    def v_arrived(t):
        kv_remote(t, 1).wait_recv()

    def kv_out(t):
        for j in range(2):
            if t <= MIRROR[t]:
                for m in sorted({t, MIRROR[t]}):
                    kv_local(m, j).wait()
            kv_remote(t, j).start()

    q_copies[0].start()
    q_copies[1].start()
    kv_out(0)
    for t in range(2, 7):
        for j in range(2):
            kv_local(t, j).start()
    kv_out(1)

    for copy in own_copies:
        copy.wait()
    q_rows = heads_in_rows(own_q[...])
    s = lax.dot_general(suffix_k[...], q_rows, NT, preferred_element_type=F32)
    u = lax.broadcasted_iota(jnp.int32, (LS, W), 0)
    t = lax.broadcasted_iota(jnp.int32, (LS, W), 1) % LS
    s = jnp.where(u <= t, s, -1e30)
    peak = jnp.max(s, axis=0, keepdims=True)
    p = jnp.exp2((s - peak) * SCALE)
    under = jnp.sum(p, axis=0, keepdims=True)
    total[...] = lax.dot_general(suffix_v[...], p.astype(BF16), TN, preferred_element_type=F32)
    for i in range(HERE):
        stats[i : i + 1, :] = peak[:, i * LS : (i + 1) * LS]
        stats[HERE + i : HERE + i + 1, :] = under[:, i * LS : (i + 1) * LS]

    q_copies[0].wait_send()
    q_copies[2].start()

    values_t[HD:, :] = jnp.ones((ONES, KEYS), BF16)
    queries[0] = own_q[...]

    def out_copies(t):
        target = device(pick(STEP, t), pick(SENT_TO, t), core)
        return [
            remote(parts.at[t], got.at[t], o_send.at[t], o_recv.at[t], target),
            remote(part_stats.at[t], got_stats.at[t], s_send.at[t], s_recv.at[t], target),
        ]

    def add(pieces, k):
        lanes = slice(k * LS, (k + 1) * LS)
        peaks = [at[k : k + 1, :] for _, at in pieces]
        highest = functools.reduce(jnp.maximum, peaks)
        over, under = 0.0, 0.0
        for (part, at), peak in zip(pieces, peaks, strict=True):
            weight = jnp.exp2((peak - highest) * SCALE)
            over = over + part[:, lanes].astype(F32) * weight
            under = under + at[HERE + k : HERE + k + 1, :] * weight
        return over, under, highest

    def fold(pieces, part, at):
        for k in range(HERE):
            over, under, highest = add(pieces, k)
            part[:, k * LS : (k + 1) * LS] = over.astype(part.dtype)
            at[k : k + 1, :] = highest
            at[HERE + k : HERE + k + 1, :] = under

    def arrived(ts):
        for t in ts:
            for copy in out_copies(t):
                copy.wait_recv()
        return [(got.at[t], got_stats.at[t]) for t in ts]

    chunks = [slice(k, k + CHUNK) for k in range(0, KEYS, CHUNK)]
    halves = [slice(0, W // 2), slice(W // 2, W)]

    def tile(t, carry):
        k_arrived(t)

        @pl.when(t == 0)
        def _():
            kv_out(2)
            kv_out(3)
            q_arrived(1)
            q_copies[3].start()
            q_copies[4].start()

        @pl.when(t == 1)
        def _():
            kv_out(4)
            kv_out(5)

        @pl.when(t == 2)
        def _():
            q_arrived(2)
            q_copies[6].start()
            kv_out(6)
            kv_out(7)

        @pl.when((t == 3) | (t == 4) | (t == 5) | (t == 7))
        def _():
            q_arrived(t)

        q_rows = heads_in_rows(queries[t])

        def score(n, at):
            s = lax.dot_general(keys[t, at, :], q_rows[halves[n]], NT, preferred_element_type=F32)
            scores[at, halves[n]] = s
            return jnp.max(s, axis=0, keepdims=True)

        def soften(n, peak, at):
            probs[at, halves[n]] = jnp.exp2((scores[at, halves[n]] - peak) * SCALE).astype(BF16)

        def finish(n, peak):
            sums = jnp.dot(values_t[...], probs[:, halves[n]], preferred_element_type=F32)
            parts[t, :, halves[n]] = sums[:HD].astype(BF16)
            for k in range(HERE // 2):
                at, head = slice(k * LS, (k + 1) * LS), n * HERE // 2 + k
                part_stats[t, head : head + 1, :] = peak[:, at]
                part_stats[t, HERE + head : HERE + head + 1, :] = sums[HD : HD + 1, at]

        peak = functools.reduce(jnp.maximum, [score(0, at) for at in chunks])
        v_arrived(t)
        values_t[:HD, :] = values[t].T
        next_peak = []
        for at in chunks:
            next_peak.append(score(1, at))
            soften(0, peak, at)
        next_peak = functools.reduce(jnp.maximum, next_peak)

        @pl.when(t == 7)
        def _():
            near = parts.at[6], part_stats.at[6]
            fold([near] + arrived((3, 4)), *near)
            for copy in out_copies(6):
                copy.start()

        finish(0, peak)
        for at in chunks:
            soften(1, next_peak, at)
        finish(1, next_peak)

        @pl.when((t != 0) & (t != 6))
        def _():
            for copy in out_copies(t):
                copy.start()

        @pl.when(t == 0)
        def _():
            q_arrived(6)
            q_copies[5].start()

        return carry

    lax.fori_loop(0, TILES, tile, 0)

    so_far = total, stats
    fold([so_far, (parts.at[0], part_stats.at[0])] + arrived((1, 2)), *so_far)
    fold([so_far] + arrived((7,)), *so_far)
    pieces = [so_far] + arrived((5, 6))
    live = lax.broadcasted_iota(jnp.int32, (LS, HD), 0) < len_ref[0]
    for k in range(HERE):
        over, under, _ = add(pieces, k)
        mixed = (over * (1.0 / under)).T
        out_ref[:, k * HD : (k + 1) * HD] = jnp.where(live, mixed, 0.0).astype(BF16)

    for copy in q_copies[1:]:
        copy.wait_send()
    for t in range(TILES):
        for j in range(2):
            kv_remote(t, j).wait_send()
        if t > 0:
            for copy in out_copies(t):
                copy.wait_send()


def on_device(queries, suffix_keys, suffix_values, prefix_keys, prefix_values, lengths):
    hbm = pl.BlockSpec(memory_space=pl.ANY)
    dma = pltpu.SemaphoreType.DMA
    out = pl.pallas_call(
        kernel,
        name="attend",
        out_shape=jax.ShapeDtypeStruct((LS, HERE * HD), BF16),
        in_specs=[hbm] * 5 + [pl.BlockSpec(memory_space=pltpu.SMEM)],
        out_specs=pl.BlockSpec(memory_space=pltpu.VMEM),
        scratch_shapes=[
            pltpu.VMEM((LS, HERE * HD), BF16),
            pltpu.VMEM((LS, HD), BF16),
            pltpu.VMEM((LS, HD), BF16),
            pltpu.VMEM((TILES, KEYS, HD), BF16),
            pltpu.VMEM((TILES, KEYS, HD), BF16),
            pltpu.VMEM((HD + ONES, KEYS), BF16),
            pltpu.VMEM((TILES, LS, HERE * HD), BF16),
            pltpu.VMEM((KEYS, W), F32),
            pltpu.VMEM((KEYS, W), BF16),
            pltpu.VMEM((TILES, HD, W), BF16),
            pltpu.VMEM((TILES, 2 * HERE, LS), F32),
            pltpu.VMEM((TILES, HD, W), BF16),
            pltpu.VMEM((TILES, 2 * HERE, LS), F32),
            pltpu.VMEM((HD, W), F32),
            pltpu.VMEM((2 * HERE, LS), F32),
            dma((3,)),
            dma((TILES, 2)),
            dma((TILES, 2)),
            dma((TILES, 2)),
            dma((7,)),
            dma((TILES,)),
            dma((TILES,)),
            dma((TILES,)),
            dma((TILES,)),
            dma((TILES,)),
        ],
        compiler_params=pltpu.CompilerParams(
            collective_id=0, has_side_effects=True, vmem_limit_bytes=62 * 2**20
        ),
        cost_estimate=pl.CostEstimate(
            flops=4 * 8192 * 1024 * 128, bytes_accessed=6 * 2**20, transcendentals=8192 * 1024
        ),
    )(
        queries.reshape(LS, HERE * HD),
        suffix_keys.reshape(LS, KVH * HD),
        suffix_values.reshape(LS, KVH * HD),
        prefix_keys,
        prefix_values,
        lengths,
    )
    return out.reshape(1, LS, HERE * HD)


def solution(mesh):
    in_specs = (
        P("cand", None, "ctx"),
        P("cand", None, None),
        P("cand", None, None),
        P("ctx", None),
        P("ctx", None),
        P("cand"),
    )
    return jax.shard_map(
        on_device, mesh=mesh, in_specs=in_specs, out_specs=P("cand", None, "ctx"), check_vma=False
    )
```
